32 devices in a mesh: seq: 16 (over z, y, core), head: 2 (over x).
Axes of the slice: x: 2, y: 2, z: 4, core: 2. Of those that a mesh axis runs over, the one named last changes fastest.
Arguments:
- queries: bfloat16 [11264, 8192], P('seq', 'head'), may hold values from -90 to 90
- encoded: bfloat16 [352, 32, 1024], P('seq', None, 'head'), may hold values from -6 to 6
- enc_gain: float32 [1024], P('head'), may hold values from 0.1 to 1.9
- w_kv: bfloat16 [1024, 2, 8192], P('seq', None, 'head'), may hold values from -0.1875 to 0.1875
- neighbour_block: int32 [352], replicated, may hold values from 0 to 175, as said below
- grad_context: bfloat16 [11264, 8192], P('seq', 'head'), may hold values from -6 to 6
Outputs:
- grad_queries: bfloat16 [11264, 8192], P('seq', 'head')
- grad_encoded: bfloat16 [352, 32, 1024], P('seq', None, 'head')
The draws below stay inside these ranges and needn't reach their ends.
Inputs may be any that keep to these rules, and one draw needn't show every extreme that they name: `neighbour_block`: every query block has exactly 2 neighbours. The 22 neighbours of one shard of encoded go to 11 distinct owners of query blocks (block // 11), exactly 2 to each.
All inputs are finite; a program needn't handle non-finite values.
Results may differ from the reference program's by a relative error of at most 0.0065.
The reference program's roundings to bfloat16 on the way (of `normed`, `probs_low`, `dscores` and `grad_normed`) count: a program that leaves them out, or rounds other values in their place, can miss the bound.
Values may be sent and summed in bfloat16 or wider, within the bound.
A program may use at most 192 MiB of HBM per device.

```python
import jax
import jax.numpy as jnp
from jax import lax

D = 8192
HEADS = 64
HEAD_DIM = 128
EW = 1024
SPAN = 64
NLEN = 32
NB = 2
TOKENS = 11264
SPAN_DEV = 11
NEIGH_DEV = 22
CAP = 2
NEIGH = 352


def draw_neighbour_block(key, part):
    first_key = jax.random.fold_in(key, 11)
    second_key = jax.random.fold_in(key, 12)
    devices = NEIGH // NEIGH_DEV
    device_order = jax.random.permutation(first_key, devices)
    owner_perms = jax.vmap(lambda sub_key: jax.random.permutation(sub_key, NEIGH_DEV))(jax.random.split(second_key, devices))
    index = jnp.arange(NEIGH, dtype=jnp.int32)
    source = index // NEIGH_DEV
    within = index % NEIGH_DEV
    target = (device_order[source] + within // CAP) % devices
    chosen = target * SPAN_DEV + owner_perms[target, within] // NB
    return chosen.astype(jnp.int32)


def draw_queries(key, part):
    base = jnp.clip(jax.random.normal(key, (TOKENS, D), jnp.float32), -6.0, 6.0)
    return base.astype(jnp.bfloat16)


def block_levels(stream_key, extent, cuts, least, top_value):
    loudness = 1.0
    for dim, shards_of in cuts:
        steps = jax.random.uniform(jax.random.fold_in(jax.random.fold_in(stream_key, 6), dim), (shards_of,), jnp.float32, least / len(cuts), top_value / len(cuts))
        loudness = loudness * jnp.repeat(jnp.exp(steps), extent[dim] // shards_of).reshape((-1,) + (1,) * (len(extent) - 1 - dim))
    return loudness


def noise(stream_key, dims, spread, reach, shards=(), held_as=jnp.bfloat16):
    gain = block_levels(stream_key, dims, shards, -0.22, 0.18) if shards else 1.0
    array = jax.random.normal(stream_key, dims, jnp.float32) * spread * gain
    return jnp.minimum(jnp.maximum(array, -reach), reach).astype(held_as)


def setup_inputs(seed: int = 0) -> dict:
    key_list = jax.random.split(jax.random.key(seed), 7)
    queries = draw_queries(jax.random.fold_in(key_list[6], 71), 0)
    encoded = noise(key_list[1], (NEIGH, NLEN, EW), 1.0, 6.0, ((0, 16), (2, 2)))
    enc_gain = jnp.clip(1.0 + 0.18 * jax.random.normal(key_list[2], (EW,), jnp.float32), 0.1, 1.9)
    w_kv = noise(key_list[3], (EW, 2, D), EW ** -0.5, 0.1875, ((0, 16), (2, 2)))
    neighbour_block = draw_neighbour_block(jax.random.fold_in(key_list[6], 71), 0)
    grad_context = noise(key_list[5], (TOKENS, D), 1.0, 6.0, ((0, 16), (1, 2)))
    return {"queries": queries, "encoded": encoded, "enc_gain": enc_gain, "w_kv": w_kv, "neighbour_block": neighbour_block, "grad_context": grad_context}


def block_ranks(neighbour_block):
    index = jnp.arange(neighbour_block.shape[0], dtype=jnp.int32)
    same_block = neighbour_block[:, None] == neighbour_block[None, :]
    earlier = index[None, :] < index[:, None]
    return lax.optimization_barrier(jnp.sum(jnp.logical_and(same_block, earlier), axis=1)).astype(jnp.int32)

def reference(queries, encoded, enc_gain, w_kv, neighbour_block, grad_context):
    scale = 1.0 / HEAD_DIM ** 0.5
    x_full = encoded.astype(jnp.float32)
    inv_rms = lax.rsqrt(lax.optimization_barrier(jnp.mean(x_full * x_full, axis=-1, keepdims=True)) + 1e-05)
    normed = (x_full * inv_rms * enc_gain).astype(jnp.bfloat16)
    position = (neighbour_block * NB + block_ranks(neighbour_block)).astype(jnp.int32)
    ordering = jnp.zeros((NEIGH,), jnp.int32).at[position].set(jnp.arange(NEIGH, dtype=jnp.int32))
    ordered = normed[ordering].reshape(NEIGH // NB, NB * NLEN, EW)
    q_blocks = queries.reshape(NEIGH // NB, SPAN, D)
    g_blocks = grad_context.reshape(NEIGH // NB, SPAN, D)

    def one_block(items):
        q_rows, g_rows, e_rows = items
        keys = jnp.dot(e_rows, w_kv[:, 0, :], preferred_element_type=jnp.float32).astype(jnp.bfloat16)
        values = jnp.dot(e_rows, w_kv[:, 1, :], preferred_element_type=jnp.float32).astype(jnp.bfloat16)
        q_heads = q_rows.astype(jnp.float32).reshape(SPAN, HEADS, HEAD_DIM)
        k_heads = keys.astype(jnp.float32).reshape(NB * NLEN, HEADS, HEAD_DIM)
        v_heads = values.astype(jnp.float32).reshape(NB * NLEN, HEADS, HEAD_DIM)
        scores = jnp.einsum('qhd,khd->hqk', q_heads, k_heads) * scale
        probs = jax.nn.softmax(scores, axis=-1)
        probs_low = probs.astype(jnp.bfloat16).astype(jnp.float32)
        g_heads = g_rows.astype(jnp.float32).reshape(SPAN, HEADS, HEAD_DIM)
        dprobs = jnp.einsum('qhd,khd->hqk', g_heads, v_heads)
        delta = lax.optimization_barrier(jnp.sum(probs * dprobs, axis=-1, keepdims=True))
        dscores = (probs * (dprobs - delta)).astype(jnp.bfloat16).astype(jnp.float32)
        grad_q = (jnp.einsum('hqk,khd->qhd', dscores, k_heads) * scale).astype(jnp.bfloat16).reshape(SPAN, D)
        grad_k = (jnp.einsum('hqk,qhd->khd', dscores, q_heads) * scale).astype(jnp.bfloat16).reshape(NB * NLEN, D)
        grad_v = jnp.einsum('hqk,qhd->khd', probs_low, g_heads).astype(jnp.bfloat16).reshape(NB * NLEN, D)
        grad_e = jnp.dot(grad_k, w_kv[:, 0, :].T, preferred_element_type=jnp.float32)
        grad_e = grad_e + jnp.dot(grad_v, w_kv[:, 1, :].T, preferred_element_type=jnp.float32)
        return (grad_q, grad_e.astype(jnp.bfloat16))
    grad_queries, grad_ordered = lax.map(one_block, (q_blocks, g_blocks, ordered))
    grad_normed = grad_ordered.reshape(NEIGH, NLEN, EW)[position].astype(jnp.float32)
    scaled = enc_gain * grad_normed
    inner = lax.optimization_barrier(jnp.mean(x_full * scaled, axis=-1, keepdims=True))
    grad_encoded = (inv_rms * scaled - x_full * inv_rms * inv_rms * inv_rms * inner).astype(jnp.bfloat16)
    return (grad_queries.reshape(TOKENS, D), grad_encoded)
```

```python
import functools

import jax
import jax.numpy as jnp
from jax import lax
from jax.experimental import pallas as pl
from jax.experimental.pallas import tpu as pltpu
from jax.sharding import PartitionSpec as P

HEAD_DIM = 128
SPAN = 64
NB = 2


def routing(neighbour_block, device, n_seq, per_dev, blocks_dev, slot_cap):
    count_all = neighbour_block.shape[0]
    index = jnp.arange(count_all, dtype=jnp.int32)
    source = index // per_dev
    holder = neighbour_block // blocks_dev
    earlier = index[None, :] < index[:, None]
    same_pair = jnp.logical_and(
        source[:, None] == source[None, :], holder[:, None] == holder[None, :]
    )
    slot_rank = jnp.sum(jnp.logical_and(same_pair, earlier), axis=1)
    block_rank = jnp.sum(
        jnp.logical_and(neighbour_block[:, None] == neighbour_block[None, :], earlier), axis=1
    )
    row_here = (neighbour_block - device * blocks_dev) * NB + block_rank
    mine_here = holder == device
    rows_local = jnp.arange(per_dev, dtype=jnp.int32)
    slots_all = jnp.arange(n_seq * slot_cap, dtype=jnp.int32)
    select_all = jnp.logical_and(
        rows_local[:, None] == row_here[None, :], mine_here[None, :]
    ).astype(jnp.bfloat16)
    slot_table = ((source * slot_cap + slot_rank)[:, None] == slots_all[None, :]).astype(
        jnp.bfloat16
    )
    recv_select = jnp.dot(select_all, slot_table, preferred_element_type=jnp.float32).astype(
        jnp.bfloat16
    )
    send_target = lax.dynamic_slice_in_dim(holder * slot_cap + slot_rank, device * per_dev, per_dev)
    send_select = (slots_all[:, None] == send_target[None, :]).astype(jnp.bfloat16)
    return (send_select, recv_select, select_all)


ACROSS = 4
CORES = 2


def gather_kernel(n, w_ref, out_ref, own_sem, send_sem, recv_sem):
    me = lax.axis_index("seq")
    wide = n // (ACROSS * CORES)
    c = lax.rem(me, CORES)
    b = lax.rem(me // CORES, wide)
    a = me // (CORES * wide)

    def at(aa, bb, cc):
        return (aa * wide + bb) * CORES + cc

    barrier = pltpu.get_barrier_semaphore()
    partners = [at(lax.rem(a + 1, ACROSS), b, c), at(lax.rem(a + ACROSS - 1, ACROSS), b, c)]
    partners.append(at(a, lax.rem(b + 1, wide), c))
    if wide > 2:
        partners.append(at(a, lax.rem(b + wide - 1, wide), c))
    partners.append(at(a, b, 1 - c))
    for partner in partners:
        pl.semaphore_signal(
            barrier, inc=1, device_id={"seq": partner}, device_id_type=pl.DeviceIdType.MESH
        )
    pl.semaphore_wait(barrier, len(partners))

    def copy(slot, way, target, own):
        return pltpu.make_async_remote_copy(
            src_ref=w_ref if own else out_ref.at[slot],
            dst_ref=out_ref.at[slot],
            send_sem=send_sem.at[way, slot],
            recv_sem=recv_sem.at[slot],
            device_id={"seq": target},
            device_id_type=pl.DeviceIdType.MESH,
        )

    def moves(aa, bb, from_a, from_b, own, act):
        slot = at(aa, bb, c)
        if from_b == 0:
            if from_a >= 0:

                @pl.when(a + 1 < ACROSS)
                def _():
                    act(copy(slot, 0, at(a + 1, b, c), own))

            if from_a <= 0:

                @pl.when(a > 0)
                def _():
                    act(copy(slot, 1, at(a - 1, b, c), own))

        if from_b >= 0:

            @pl.when(b + 1 < wide)
            def _():
                act(copy(slot, 2, at(a, b + 1, c), own))

        if from_b <= 0:

            @pl.when(b > 0)
            def _():
                act(copy(slot, 3, at(a, b - 1, c), own))

        act(copy(slot, 4, at(a, b, 1 - c), own))

    def start(item):
        item.start()

    def wait_recv(slot):
        copy(slot, 4, at(a, b, 1 - c), False).wait_recv()

    def visit(each):
        for t in range(1, ACROSS + wide - 1):
            for j in range(0, min(t, wide - 1) + 1):
                k = t - j
                if k > ACROSS - 1:
                    continue
                for sa in (1, -1) if k else (0,):
                    for sb in (1, -1) if j else (0,):
                        aa, bb = a - sa * k, b - sb * j
                        here = None
                        if sa:
                            here = aa >= 0 if sa > 0 else aa < ACROSS
                        if sb:
                            more = bb >= 0 if sb > 0 else bb < wide
                            here = more if here is None else jnp.logical_and(here, more)

                        @pl.when(here)
                        def _(aa=aa, bb=bb, sa=sa, sb=sb):
                            each(aa, bb, sa, sb)

    own_copy = pltpu.make_async_copy(w_ref, out_ref.at[me], own_sem)
    moves(a, b, 0, 0, True, start)
    own_copy.start()

    def forward(aa, bb, sa, sb):
        wait_recv(at(aa, bb, c))
        moves(aa, bb, sa, sb, False, start)

    visit(forward)
    for aa in range(ACROSS):
        for bb in range(wide):
            wait_recv(at(aa, bb, 1 - c))
    own_copy.wait()
    moves(a, b, 0, 0, True, lambda item: item.wait_send())
    visit(lambda aa, bb, sa, sb: moves(aa, bb, sa, sb, False, lambda item: item.wait_send()))


def gather_weights(weights):
    n = lax.axis_size("seq")
    return pl.pallas_call(
        functools.partial(gather_kernel, n),
        out_shape=jax.ShapeDtypeStruct((n,) + weights.shape, weights.dtype),
        in_specs=[pl.BlockSpec(memory_space=pl.ANY)],
        out_specs=pl.BlockSpec(memory_space=pl.ANY),
        scratch_shapes=[
            pltpu.SemaphoreType.DMA,
            pltpu.SemaphoreType.DMA((5, n)),
            pltpu.SemaphoreType.DMA((n,)),
        ],
        compiler_params=pltpu.CompilerParams(collective_id=0, has_side_effects=True),
    )(weights)


GROUP = 4


def attention_kernel(q_ref, g_ref, kv_ref, gq_ref, gkv_ref):
    d_part = q_ref.shape[1]
    scale = 1.0 / HEAD_DIM**0.5
    nt = (((1,), (1,)), ((), ()))
    tn = (((0,), (0,)), ((), ()))
    dot = functools.partial(lax.dot_general, preferred_element_type=jnp.float32)

    @pl.loop(0, d_part // (GROUP * HEAD_DIM))
    def _(step):
        for h in range(GROUP):
            start = pl.multiple_of((step * GROUP + h) * HEAD_DIM, HEAD_DIM)
            cols = pl.ds(start, HEAD_DIM)
            cols_v = pl.ds(pl.multiple_of(start + d_part, HEAD_DIM), HEAD_DIM)
            q, g = q_ref[:, cols], g_ref[:, cols]
            k, v = kv_ref[:, cols], kv_ref[:, cols_v]
            scores = dot(q, k, nt) * scale
            weight = jnp.exp(scores - jnp.max(scores, axis=-1, keepdims=True))
            probs = weight / jnp.sum(weight, axis=-1, keepdims=True)
            dprobs = dot(g, v, nt)
            delta = jnp.sum(probs * dprobs, axis=-1, keepdims=True)
            dscores = (probs * (dprobs - delta)).astype(jnp.bfloat16)
            low = probs.astype(jnp.bfloat16)
            gq_ref[:, cols] = (jnp.dot(dscores, k, preferred_element_type=jnp.float32) * scale).astype(
                jnp.bfloat16
            )
            gkv_ref[:, cols] = (dot(dscores, q, tn) * scale).astype(jnp.bfloat16)
            gkv_ref[:, cols_v] = dot(low, g, tn).astype(jnp.bfloat16)


def attention(queries, grads, kv):
    rows, d_part = queries.shape
    keys_rows = kv.shape[0] * SPAN // rows

    def spec(height, width):
        return pl.BlockSpec((height, width), lambda i: (i, 0))

    return pl.pallas_call(
        attention_kernel,
        grid=(rows // SPAN,),
        out_shape=(
            jax.ShapeDtypeStruct(queries.shape, jnp.bfloat16),
            jax.ShapeDtypeStruct(kv.shape, jnp.bfloat16),
        ),
        in_specs=[spec(SPAN, d_part), spec(SPAN, d_part), spec(keys_rows, 2 * d_part)],
        out_specs=(spec(SPAN, d_part), spec(keys_rows, 2 * d_part)),
        compiler_params=pltpu.CompilerParams(vmem_limit_bytes=40 * 1024 * 1024),
    )(queries, grads, kv)


def shards(queries, encoded, enc_gain, w_kv, neighbour_block, grad_context):
    n_seq = lax.axis_size("seq")
    device = lax.axis_index("seq")
    per_dev, nlen, ew_part = encoded.shape
    ew_full = ew_part * lax.axis_size("head")
    tok_rows, d_part = queries.shape
    blocks_dev = tok_rows // SPAN
    slot_cap = (per_dev + n_seq - 1) // n_seq
    x_part = encoded.astype(jnp.float32)
    squares = lax.psum(jnp.sum(x_part * x_part, axis=-1), "head")
    inv_rms = lax.rsqrt(squares / ew_full + 1e-05)[..., None]
    normed = (x_part * inv_rms * enc_gain).astype(jnp.bfloat16)
    send_select, recv_select, select_all = routing(
        neighbour_block, device, n_seq, per_dev, blocks_dev, slot_cap
    )
    width_row = nlen * ew_part
    outgoing = jnp.dot(
        send_select, normed.reshape(per_dev, width_row), preferred_element_type=jnp.float32
    )
    outgoing = outgoing.astype(jnp.bfloat16).reshape(n_seq, slot_cap * width_row)
    incoming = lax.all_to_all(outgoing, "seq", split_axis=0, concat_axis=0, tiled=True)
    gathered = jnp.dot(
        recv_select,
        incoming.reshape(n_seq * slot_cap, width_row),
        preferred_element_type=jnp.float32,
    )
    owned = gathered.astype(jnp.bfloat16).reshape(per_dev, nlen, ew_part)
    full_rows = lax.all_gather(owned, "head", axis=2, tiled=True).reshape(per_dev * nlen, ew_full)
    flat = w_kv.reshape(w_kv.shape[0], 2 * d_part)
    weights = gather_weights(flat).reshape(ew_full, 2 * d_part)
    kv = jnp.dot(full_rows, weights, preferred_element_type=jnp.float32).astype(jnp.bfloat16)
    grad_queries, grad_kv = attention(queries, grad_context, kv)
    partial_rows = lax.dot_general(
        grad_kv, weights, (((1,), (1,)), ((), ())), preferred_element_type=jnp.float32
    )
    summed = lax.psum_scatter(
        partial_rows.reshape(per_dev, nlen, ew_full), "head", scatter_dimension=2, tiled=True
    )
    grad_owned = summed.astype(jnp.bfloat16).reshape(per_dev, width_row)
    returning = jnp.dot(recv_select.T, grad_owned, preferred_element_type=jnp.float32)
    returning = returning.astype(jnp.bfloat16).reshape(n_seq, slot_cap * width_row)
    arrived = lax.all_to_all(returning, "seq", split_axis=0, concat_axis=0, tiled=True)
    grad_normed = jnp.dot(
        send_select.T,
        arrived.reshape(n_seq * slot_cap, width_row),
        preferred_element_type=jnp.float32,
    )
    grad_normed = grad_normed.reshape(per_dev, nlen, ew_part)
    scaled = enc_gain * grad_normed
    inner = lax.psum(jnp.sum(x_part * scaled, axis=-1), "head")[..., None] / ew_full
    grad_encoded = (inv_rms * scaled - x_part * inv_rms * inv_rms * inv_rms * inner).astype(
        jnp.bfloat16
    )
    return (grad_queries, grad_encoded)


def solution(mesh):
    return jax.shard_map(
        shards,
        mesh=mesh,
        in_specs=(
            P("seq", "head"),
            P("seq", None, "head"),
            P("head"),
            P("seq", None, "head"),
            P(),
            P("seq", "head"),
        ),
        out_specs=(P("seq", "head"), P("seq", None, "head")),
        check_vma=False,
    )
```

```python
import functools

import jax
import jax.numpy as jnp
from jax import lax
from jax.experimental import pallas as pl
from jax.experimental.pallas import tpu as pltpu
from jax.sharding import PartitionSpec as P

HEAD_DIM = 128
SPAN = 64
NB = 2


def routing(neighbour_block, device, n_seq, per_dev, blocks_dev, slot_cap):
    count_all = neighbour_block.shape[0]
    index = jnp.arange(count_all, dtype=jnp.int32)
    source = index // per_dev
    holder = neighbour_block // blocks_dev
    earlier = index[None, :] < index[:, None]
    same_pair = jnp.logical_and(
        source[:, None] == source[None, :], holder[:, None] == holder[None, :]
    )
    slot_rank = jnp.sum(jnp.logical_and(same_pair, earlier), axis=1)
    block_rank = jnp.sum(
        jnp.logical_and(neighbour_block[:, None] == neighbour_block[None, :], earlier), axis=1
    )
    row_here = (neighbour_block - device * blocks_dev) * NB + block_rank
    mine_here = holder == device
    rows_local = jnp.arange(per_dev, dtype=jnp.int32)
    slots_all = jnp.arange(n_seq * slot_cap, dtype=jnp.int32)
    select_all = jnp.logical_and(
        rows_local[:, None] == row_here[None, :], mine_here[None, :]
    ).astype(jnp.bfloat16)
    slot_table = ((source * slot_cap + slot_rank)[:, None] == slots_all[None, :]).astype(
        jnp.bfloat16
    )
    recv_select = jnp.dot(select_all, slot_table, preferred_element_type=jnp.float32).astype(
        jnp.bfloat16
    )
    send_target = lax.dynamic_slice_in_dim(holder * slot_cap + slot_rank, device * per_dev, per_dev)
    send_select = (slots_all[:, None] == send_target[None, :]).astype(jnp.bfloat16)
    return (send_select, recv_select, select_all)


ACROSS = 4
CORES = 2


def gather_kernel(n, w_ref, out_ref, own_sem, send_sem, recv_sem):
    me = lax.axis_index("seq")
    wide = n // (ACROSS * CORES)
    c = lax.rem(me, CORES)
    b = lax.rem(me // CORES, wide)
    a = me // (CORES * wide)

    def at(aa, bb, cc):
        return (aa * wide + bb) * CORES + cc

    barrier = pltpu.get_barrier_semaphore()
    partners = [at(lax.rem(a + 1, ACROSS), b, c), at(lax.rem(a + ACROSS - 1, ACROSS), b, c)]
    partners.append(at(a, lax.rem(b + 1, wide), c))
    if wide > 2:
        partners.append(at(a, lax.rem(b + wide - 1, wide), c))
    partners.append(at(a, b, 1 - c))
    for partner in partners:
        pl.semaphore_signal(
            barrier, inc=1, device_id={"seq": partner}, device_id_type=pl.DeviceIdType.MESH
        )
    pl.semaphore_wait(barrier, len(partners))

    def copy(slot, way, target, own):
        return pltpu.make_async_remote_copy(
            src_ref=w_ref if own else out_ref.at[slot],
            dst_ref=out_ref.at[slot],
            send_sem=send_sem.at[way, slot],
            recv_sem=recv_sem.at[slot],
            device_id={"seq": target},
            device_id_type=pl.DeviceIdType.MESH,
        )

    def moves(aa, bb, from_a, from_b, own, act):
        slot = at(aa, bb, c)
        if from_b == 0:
            if from_a >= 0:

                @pl.when(a + 1 < ACROSS)
                def _():
                    act(copy(slot, 0, at(a + 1, b, c), own))

            if from_a <= 0:

                @pl.when(a > 0)
                def _():
                    act(copy(slot, 1, at(a - 1, b, c), own))

        if from_b >= 0:

            @pl.when(b + 1 < wide)
            def _():
                act(copy(slot, 2, at(a, b + 1, c), own))

        if from_b <= 0:

            @pl.when(b > 0)
            def _():
                act(copy(slot, 3, at(a, b - 1, c), own))

        act(copy(slot, 4, at(a, b, 1 - c), own))

    def start(item):
        item.start()

    def wait_recv(slot):
        copy(slot, 4, at(a, b, 1 - c), False).wait_recv()

    def visit(each):
        for t in range(1, ACROSS + wide - 1):
            for j in range(0, min(t, wide - 1) + 1):
                k = t - j
                if k > ACROSS - 1:
                    continue
                for sa in (1, -1) if k else (0,):
                    for sb in (1, -1) if j else (0,):
                        aa, bb = a - sa * k, b - sb * j
                        here = None
                        if sa:
                            here = aa >= 0 if sa > 0 else aa < ACROSS
                        if sb:
                            more = bb >= 0 if sb > 0 else bb < wide
                            here = more if here is None else jnp.logical_and(here, more)

                        @pl.when(here)
                        def _(aa=aa, bb=bb, sa=sa, sb=sb):
                            each(aa, bb, sa, sb)

    own_copy = pltpu.make_async_copy(w_ref, out_ref.at[me], own_sem)
    moves(a, b, 0, 0, True, start)
    own_copy.start()

    def forward(aa, bb, sa, sb):
        wait_recv(at(aa, bb, c))
        moves(aa, bb, sa, sb, False, start)

    visit(forward)
    for aa in range(ACROSS):
        for bb in range(wide):
            wait_recv(at(aa, bb, 1 - c))
    own_copy.wait()
    moves(a, b, 0, 0, True, lambda item: item.wait_send())
    visit(lambda aa, bb, sa, sb: moves(aa, bb, sa, sb, False, lambda item: item.wait_send()))


def gather_weights(weights):
    n = lax.axis_size("seq")
    return pl.pallas_call(
        functools.partial(gather_kernel, n),
        out_shape=jax.ShapeDtypeStruct((n,) + weights.shape, weights.dtype),
        in_specs=[pl.BlockSpec(memory_space=pl.ANY)],
        out_specs=pl.BlockSpec(memory_space=pl.ANY),
        scratch_shapes=[
            pltpu.SemaphoreType.DMA,
            pltpu.SemaphoreType.DMA((5, n)),
            pltpu.SemaphoreType.DMA((n,)),
        ],
        compiler_params=pltpu.CompilerParams(collective_id=0, has_side_effects=True),
    )(weights)


GROUP = 4


def attention_kernel(q_ref, g_ref, kv_ref, gq_ref, gkv_ref):
    d_part = q_ref.shape[1]
    pair = 2 * HEAD_DIM
    scale = 1.0 / HEAD_DIM**0.5
    nt = (((1,), (1,)), ((), ()))
    tn = (((0,), (0,)), ((), ()))
    dot = functools.partial(lax.dot_general, preferred_element_type=jnp.float32)

    def diagonal(x):
        blank = jnp.zeros((x.shape[0], HEAD_DIM), x.dtype)
        upper = jnp.concatenate([x[:, :HEAD_DIM], blank], axis=1)
        lower = jnp.concatenate([blank, x[:, HEAD_DIM:]], axis=1)
        return jnp.concatenate([upper, lower], axis=0)

    @pl.loop(0, d_part // (GROUP * pair))
    def _(step):
        cols, cols_v = [], []
        for h in range(GROUP):
            start = pl.multiple_of((step * GROUP + h) * pair, pair)
            cols.append(pl.ds(start, pair))
            cols_v.append(pl.ds(pl.multiple_of(start + d_part, pair), pair))
        queries = [diagonal(q_ref[:, c]) for c in cols]
        grads = [diagonal(g_ref[:, c]) for c in cols]
        keys = [kv_ref[:, c] for c in cols]
        values = [kv_ref[:, c] for c in cols_v]
        scores = [dot(k, q, nt) * scale for k, q in zip(keys, queries)]
        dprobs = [dot(v, g, nt) for v, g in zip(values, grads)]
        low, dscores = [], []
        for s, dp in zip(scores, dprobs):
            weight = jnp.exp(s - jnp.max(s, axis=0, keepdims=True))
            probs = weight / jnp.sum(weight, axis=0, keepdims=True)
            delta = jnp.sum(probs * dp, axis=0, keepdims=True)
            low.append(probs.astype(jnp.bfloat16))
            dscores.append((probs * (dp - delta)).astype(jnp.bfloat16))
        grad_k = [dot(d, q, (((1,), (0,)), ((), ()))) * scale for d, q in zip(dscores, queries)]
        grad_v = [dot(p, g, (((1,), (0,)), ((), ()))) for p, g in zip(low, grads)]
        grad_q = [dot(d, k, tn) * scale for d, k in zip(dscores, keys)]
        for h in range(GROUP):
            gkv_ref[:, cols[h]] = grad_k[h].astype(jnp.bfloat16)
            gkv_ref[:, cols_v[h]] = grad_v[h].astype(jnp.bfloat16)
            both = jnp.concatenate(
                [grad_q[h][:SPAN, :HEAD_DIM], grad_q[h][SPAN:, HEAD_DIM:]], axis=1
            )
            gq_ref[:, cols[h]] = both.astype(jnp.bfloat16)


def attention(queries, grads, kv):
    rows, d_part = queries.shape
    keys_rows = kv.shape[0] * SPAN // rows

    def spec(height, width):
        return pl.BlockSpec((height, width), lambda i: (i, 0))

    return pl.pallas_call(
        attention_kernel,
        grid=(rows // SPAN,),
        out_shape=(
            jax.ShapeDtypeStruct(queries.shape, jnp.bfloat16),
            jax.ShapeDtypeStruct(kv.shape, jnp.bfloat16),
        ),
        in_specs=[spec(SPAN, d_part), spec(SPAN, d_part), spec(keys_rows, 2 * d_part)],
        out_specs=(spec(SPAN, d_part), spec(keys_rows, 2 * d_part)),
        compiler_params=pltpu.CompilerParams(vmem_limit_bytes=40 * 1024 * 1024),
    )(queries, grads, kv)


def shards(queries, encoded, enc_gain, w_kv, neighbour_block, grad_context):
    n_seq = lax.axis_size("seq")
    device = lax.axis_index("seq")
    per_dev, nlen, ew_part = encoded.shape
    ew_full = ew_part * lax.axis_size("head")
    tok_rows, d_part = queries.shape
    blocks_dev = tok_rows // SPAN
    slot_cap = (per_dev + n_seq - 1) // n_seq
    x_part = encoded.astype(jnp.float32)
    squares = lax.psum(jnp.sum(x_part * x_part, axis=-1), "head")
    inv_rms = lax.rsqrt(squares / ew_full + 1e-05)[..., None]
    normed = (x_part * inv_rms * enc_gain).astype(jnp.bfloat16)
    send_select, recv_select, select_all = routing(
        neighbour_block, device, n_seq, per_dev, blocks_dev, slot_cap
    )
    width_row = nlen * ew_part
    outgoing = jnp.dot(
        send_select, normed.reshape(per_dev, width_row), preferred_element_type=jnp.float32
    )
    outgoing = outgoing.astype(jnp.bfloat16).reshape(n_seq, slot_cap * width_row)
    incoming = lax.all_to_all(outgoing, "seq", split_axis=0, concat_axis=0, tiled=True)
    gathered = jnp.dot(
        recv_select,
        incoming.reshape(n_seq * slot_cap, width_row),
        preferred_element_type=jnp.float32,
    )
    owned = gathered.astype(jnp.bfloat16).reshape(per_dev, nlen, ew_part)
    full_rows = lax.all_gather(owned, "head", axis=2, tiled=True).reshape(per_dev * nlen, ew_full)
    flat = w_kv.reshape(w_kv.shape[0], 2 * d_part)
    weights = gather_weights(flat).reshape(ew_full, 2 * d_part)
    kv = jnp.dot(full_rows, weights, preferred_element_type=jnp.float32).astype(jnp.bfloat16)
    grad_queries, grad_kv = attention(queries, grad_context, kv)
    partial_rows = lax.dot_general(
        grad_kv, weights, (((1,), (1,)), ((), ())), preferred_element_type=jnp.float32
    )
    summed = lax.psum_scatter(
        partial_rows.reshape(per_dev, nlen, ew_full), "head", scatter_dimension=2, tiled=True
    )
    grad_owned = summed.astype(jnp.bfloat16).reshape(per_dev, width_row)
    returning = jnp.dot(recv_select.T, grad_owned, preferred_element_type=jnp.float32)
    returning = returning.astype(jnp.bfloat16).reshape(n_seq, slot_cap * width_row)
    arrived = lax.all_to_all(returning, "seq", split_axis=0, concat_axis=0, tiled=True)
    grad_normed = jnp.dot(
        send_select.T,
        arrived.reshape(n_seq * slot_cap, width_row),
        preferred_element_type=jnp.float32,
    )
    grad_normed = grad_normed.reshape(per_dev, nlen, ew_part)
    scaled = enc_gain * grad_normed
    inner = lax.psum(jnp.sum(x_part * scaled, axis=-1), "head")[..., None] / ew_full
    grad_encoded = (inv_rms * scaled - x_part * inv_rms * inv_rms * inv_rms * inner).astype(
        jnp.bfloat16
    )
    return (grad_queries, grad_encoded)


def solution(mesh):
    return jax.shard_map(
        shards,
        mesh=mesh,
        in_specs=(
            P("seq", "head"),
            P("seq", None, "head"),
            P("head"),
            P("seq", None, "head"),
            P(),
            P("seq", "head"),
        ),
        out_specs=(P("seq", "head"), P("seq", None, "head")),
        check_vma=False,
    )
```

```python
import functools

import jax
import jax.numpy as jnp
from jax import lax
from jax.experimental import pallas as pl
from jax.experimental.pallas import tpu as pltpu
from jax.sharding import PartitionSpec as P

HEAD_DIM = 128
SPAN = 64
NB = 2


def greet(n, heads, me, hd):
    barrier = pltpu.get_barrier_semaphore()
    for d in range(1, n):
        pl.semaphore_signal(
            barrier,
            inc=1,
            device_id={"seq": lax.rem(me + d, n)},
            device_id_type=pl.DeviceIdType.MESH,
        )
    for d in range(1, heads):
        pl.semaphore_signal(
            barrier,
            inc=1,
            device_id={"head": lax.rem(hd + d, heads)},
            device_id_type=pl.DeviceIdType.MESH,
        )
    pl.semaphore_wait(barrier, n + heads - 2)


def remote(src, dst, send, recv, **place):
    return pltpu.make_async_remote_copy(
        src_ref=src,
        dst_ref=dst,
        send_sem=send,
        recv_sem=recv,
        device_id=place,
        device_id_type=pl.DeviceIdType.MESH,
    )


def fold(values):
    total = values[:, :HEAD_DIM]
    for k in range(1, values.shape[1] // HEAD_DIM):
        total = total + values[:, k * HEAD_DIM : (k + 1) * HEAD_DIM]
    return total


def tail_kernel(
    n, heads, back_ref, take_ref, partial_ref, x_ref, rms_ref, gain_ref, out_ref,
    own, land, owned, packed, arrived, mine, others,
    own_sem, rs_send, rs_recv, a_send, a_recv, s_send, s_recv,
):
    me, hd = lax.axis_index("seq"), lax.axis_index("head")
    per_dev, nlen, ew_part = x_ref.shape
    cap = packed.shape[0] // n
    greet(n, heads, me, hd)

    def piece(which):
        return partial_ref.at[:, :, pl.ds(pl.multiple_of(which * ew_part, ew_part), ew_part)]

    sums = []
    for d in range(1, heads):
        to = lax.rem(hd + d, heads)
        sums.append(
            remote(piece(to), land.at[d - 1], rs_send.at[d - 1], rs_recv.at[d - 1], head=to)
        )
        sums[-1].start()
    local = pltpu.make_async_copy(piece(hd), own, own_sem)
    local.start()
    local.wait()
    for item in sums:
        item.wait_recv()

    @pl.loop(0, per_dev)
    def _(r):
        total = own[r]
        for d in range(1, heads):
            total = total + land[d - 1, r]
        owned[r] = total.astype(jnp.bfloat16)

    def parcel(d):
        to = lax.rem(me + d, n)
        return remote(
            packed.at[pl.ds(to * cap, cap)],
            arrived.at[pl.ds(me * cap, cap)],
            a_send.at[d - 1],
            a_recv.at[d - 1],
            seq=to,
        )

    for d in range(1, n):
        to = lax.rem(me + d, n)
        for t in range(cap):
            packed[to * cap + t] = owned[back_ref[to * cap + t]]
        parcel(d).start()
    for t in range(cap):
        arrived[me * cap + t] = owned[back_ref[me * cap + t]]
    for d in range(1, n):
        parcel(d).wait_recv()

    gain = gain_ref[...]

    @pl.loop(0, per_dev)
    def _(i):
        scaled = gain * arrived[take_ref[i]].astype(jnp.float32)
        mine[i] = fold(x_ref[i].astype(jnp.float32) * scaled)

    inners = []
    for d in range(1, heads):
        to = lax.rem(hd + d, heads)
        inners.append(remote(mine, others.at[d - 1], s_send.at[d - 1], s_recv.at[d - 1], head=to))
        inners[-1].start()
    for item in inners:
        item.wait_recv()

    @pl.loop(0, per_dev)
    def _(i):
        total = mine[i]
        for d in range(1, heads):
            total = total + others[d - 1, i]
        inner = jnp.sum(total, axis=-1, keepdims=True) / (ew_part * heads)
        scaled = gain * arrived[take_ref[i]].astype(jnp.float32)
        rms = rms_ref[i]
        x = x_ref[i].astype(jnp.float32)
        out_ref[i] = (rms * scaled - x * (rms * rms * rms * inner)).astype(jnp.bfloat16)

    for item in sums + inners:
        item.wait_send()
    for d in range(1, n):
        parcel(d).wait_send()


def tail(back, take, partial, x, rms, gain):
    n, heads = lax.axis_size("seq"), lax.axis_size("head")
    per_dev, nlen, ew_part = x.shape
    vmem = pl.BlockSpec(memory_space=pltpu.VMEM)
    smem = pl.BlockSpec(memory_space=pltpu.SMEM)
    slots = back.shape[0]
    return pl.pallas_call(
        functools.partial(tail_kernel, n, heads),
        out_shape=jax.ShapeDtypeStruct(x.shape, jnp.bfloat16),
        in_specs=[smem, smem, pl.BlockSpec(memory_space=pl.ANY), vmem, vmem, vmem],
        out_specs=vmem,
        scratch_shapes=[
            pltpu.VMEM(x.shape, jnp.float32),
            pltpu.VMEM((heads - 1,) + x.shape, jnp.float32),
            pltpu.VMEM(x.shape, jnp.bfloat16),
            pltpu.VMEM((slots, nlen, ew_part), jnp.bfloat16),
            pltpu.VMEM((slots, nlen, ew_part), jnp.bfloat16),
            pltpu.VMEM((per_dev, nlen, HEAD_DIM), jnp.float32),
            pltpu.VMEM((heads - 1, per_dev, nlen, HEAD_DIM), jnp.float32),
            pltpu.SemaphoreType.DMA,
            pltpu.SemaphoreType.DMA((heads - 1,)),
            pltpu.SemaphoreType.DMA((heads - 1,)),
            pltpu.SemaphoreType.DMA((n - 1,)),
            pltpu.SemaphoreType.DMA((n - 1,)),
            pltpu.SemaphoreType.DMA((heads - 1,)),
            pltpu.SemaphoreType.DMA((heads - 1,)),
        ],
        compiler_params=pltpu.CompilerParams(
            collective_id=1, has_side_effects=True, vmem_limit_bytes=32 * 1024 * 1024
        ),
    )(back, take, partial, x, rms, gain)


def routing(neighbour_block, device, n_seq, per_dev, blocks_dev, slot_cap):
    count_all = neighbour_block.shape[0]
    index = jnp.arange(count_all, dtype=jnp.int32)
    source = index // per_dev
    holder = neighbour_block // blocks_dev
    earlier = index[None, :] < index[:, None]
    same_pair = jnp.logical_and(
        source[:, None] == source[None, :], holder[:, None] == holder[None, :]
    )
    slot_rank = jnp.sum(jnp.logical_and(same_pair, earlier), axis=1)
    block_rank = jnp.sum(
        jnp.logical_and(neighbour_block[:, None] == neighbour_block[None, :], earlier), axis=1
    )
    row_here = (neighbour_block - device * blocks_dev) * NB + block_rank
    mine_here = holder == device
    rows_local = jnp.arange(per_dev, dtype=jnp.int32)
    slots_all = jnp.arange(n_seq * slot_cap, dtype=jnp.int32)
    select_all = jnp.logical_and(
        rows_local[:, None] == row_here[None, :], mine_here[None, :]
    ).astype(jnp.bfloat16)
    slot_table = ((source * slot_cap + slot_rank)[:, None] == slots_all[None, :]).astype(
        jnp.bfloat16
    )
    recv_select = jnp.dot(select_all, slot_table, preferred_element_type=jnp.float32).astype(
        jnp.bfloat16
    )
    send_target = lax.dynamic_slice_in_dim(holder * slot_cap + slot_rank, device * per_dev, per_dev)
    send_select = (slots_all[:, None] == send_target[None, :]).astype(jnp.bfloat16)
    back_row = jnp.sum(
        recv_select.astype(jnp.int32) * rows_local[:, None], axis=0, dtype=jnp.int32
    )
    return (send_select, recv_select, send_target.astype(jnp.int32), back_row)


ACROSS = 4
CORES = 2


def gather_kernel(n, w_ref, out_ref, own_sem, send_sem, recv_sem):
    me = lax.axis_index("seq")
    wide = n // (ACROSS * CORES)
    c = lax.rem(me, CORES)
    b = lax.rem(me // CORES, wide)
    a = me // (CORES * wide)

    def at(aa, bb, cc):
        return (aa * wide + bb) * CORES + cc

    barrier = pltpu.get_barrier_semaphore()
    partners = [at(lax.rem(a + 1, ACROSS), b, c), at(lax.rem(a + ACROSS - 1, ACROSS), b, c)]
    partners.append(at(a, lax.rem(b + 1, wide), c))
    if wide > 2:
        partners.append(at(a, lax.rem(b + wide - 1, wide), c))
    partners.append(at(a, b, 1 - c))
    for partner in partners:
        pl.semaphore_signal(
            barrier, inc=1, device_id={"seq": partner}, device_id_type=pl.DeviceIdType.MESH
        )
    pl.semaphore_wait(barrier, len(partners))

    def copy(slot, way, target, own):
        return pltpu.make_async_remote_copy(
            src_ref=w_ref if own else out_ref.at[slot],
            dst_ref=out_ref.at[slot],
            send_sem=send_sem.at[way, slot],
            recv_sem=recv_sem.at[slot],
            device_id={"seq": target},
            device_id_type=pl.DeviceIdType.MESH,
        )

    def moves(aa, bb, from_a, from_b, own, act):
        slot = at(aa, bb, c)
        if from_b == 0:
            if from_a >= 0:

                @pl.when(a + 1 < ACROSS)
                def _():
                    act(copy(slot, 0, at(a + 1, b, c), own))

            if from_a <= 0:

                @pl.when(a > 0)
                def _():
                    act(copy(slot, 1, at(a - 1, b, c), own))

        if from_b >= 0:

            @pl.when(b + 1 < wide)
            def _():
                act(copy(slot, 2, at(a, b + 1, c), own))

        if from_b <= 0:

            @pl.when(b > 0)
            def _():
                act(copy(slot, 3, at(a, b - 1, c), own))

        act(copy(slot, 4, at(a, b, 1 - c), own))

    def start(item):
        item.start()

    def wait_recv(slot):
        copy(slot, 4, at(a, b, 1 - c), False).wait_recv()

    def visit(each):
        for t in range(1, ACROSS + wide - 1):
            for j in range(0, min(t, wide - 1) + 1):
                k = t - j
                if k > ACROSS - 1:
                    continue
                for sa in (1, -1) if k else (0,):
                    for sb in (1, -1) if j else (0,):
                        aa, bb = a - sa * k, b - sb * j
                        here = None
                        if sa:
                            here = aa >= 0 if sa > 0 else aa < ACROSS
                        if sb:
                            more = bb >= 0 if sb > 0 else bb < wide
                            here = more if here is None else jnp.logical_and(here, more)

                        @pl.when(here)
                        def _(aa=aa, bb=bb, sa=sa, sb=sb):
                            each(aa, bb, sa, sb)

    own_copy = pltpu.make_async_copy(w_ref, out_ref.at[me], own_sem)
    moves(a, b, 0, 0, True, start)
    own_copy.start()

    def forward(aa, bb, sa, sb):
        wait_recv(at(aa, bb, c))
        moves(aa, bb, sa, sb, False, start)

    visit(forward)
    for aa in range(ACROSS):
        for bb in range(wide):
            wait_recv(at(aa, bb, 1 - c))
    own_copy.wait()
    moves(a, b, 0, 0, True, lambda item: item.wait_send())
    visit(lambda aa, bb, sa, sb: moves(aa, bb, sa, sb, False, lambda item: item.wait_send()))


def gather_weights(weights):
    n = lax.axis_size("seq")
    return pl.pallas_call(
        functools.partial(gather_kernel, n),
        out_shape=jax.ShapeDtypeStruct((n,) + weights.shape, weights.dtype),
        in_specs=[pl.BlockSpec(memory_space=pl.ANY)],
        out_specs=pl.BlockSpec(memory_space=pl.ANY),
        scratch_shapes=[
            pltpu.SemaphoreType.DMA,
            pltpu.SemaphoreType.DMA((5, n)),
            pltpu.SemaphoreType.DMA((n,)),
        ],
        compiler_params=pltpu.CompilerParams(collective_id=0, has_side_effects=True),
    )(weights)


GROUP = 4


def attention_kernel(q_ref, g_ref, kv_ref, gq_ref, gkv_ref):
    d_part = q_ref.shape[1]
    pair = 2 * HEAD_DIM
    scale = 1.0 / HEAD_DIM**0.5
    nt = (((1,), (1,)), ((), ()))
    tn = (((0,), (0,)), ((), ()))
    dot = functools.partial(lax.dot_general, preferred_element_type=jnp.float32)

    def diagonal(x):
        blank = jnp.zeros((x.shape[0], HEAD_DIM), x.dtype)
        upper = jnp.concatenate([x[:, :HEAD_DIM], blank], axis=1)
        lower = jnp.concatenate([blank, x[:, HEAD_DIM:]], axis=1)
        return jnp.concatenate([upper, lower], axis=0)

    @pl.loop(0, d_part // (GROUP * pair))
    def _(step):
        cols, cols_v = [], []
        for h in range(GROUP):
            start = pl.multiple_of((step * GROUP + h) * pair, pair)
            cols.append(pl.ds(start, pair))
            cols_v.append(pl.ds(pl.multiple_of(start + d_part, pair), pair))
        queries = [diagonal(q_ref[:, c]) for c in cols]
        grads = [diagonal(g_ref[:, c]) for c in cols]
        keys = [kv_ref[:, c] for c in cols]
        values = [kv_ref[:, c] for c in cols_v]
        scores = [dot(k, q, nt) * scale for k, q in zip(keys, queries)]
        dprobs = [dot(v, g, nt) for v, g in zip(values, grads)]
        low, dscores = [], []
        for s, dp in zip(scores, dprobs):
            weight = jnp.exp(s - jnp.max(s, axis=0, keepdims=True))
            probs = weight / jnp.sum(weight, axis=0, keepdims=True)
            delta = jnp.sum(probs * dp, axis=0, keepdims=True)
            low.append(probs.astype(jnp.bfloat16))
            dscores.append((probs * (dp - delta)).astype(jnp.bfloat16))
        grad_k = [dot(d, q, (((1,), (0,)), ((), ()))) * scale for d, q in zip(dscores, queries)]
        grad_v = [dot(p, g, (((1,), (0,)), ((), ()))) for p, g in zip(low, grads)]
        grad_q = [dot(d, k, tn) * scale for d, k in zip(dscores, keys)]
        for h in range(GROUP):
            gkv_ref[:, cols[h]] = grad_k[h].astype(jnp.bfloat16)
            gkv_ref[:, cols_v[h]] = grad_v[h].astype(jnp.bfloat16)
            both = jnp.concatenate(
                [grad_q[h][:SPAN, :HEAD_DIM], grad_q[h][SPAN:, HEAD_DIM:]], axis=1
            )
            gq_ref[:, cols[h]] = both.astype(jnp.bfloat16)


def attention(queries, grads, kv):
    rows, d_part = queries.shape
    keys_rows = kv.shape[0] * SPAN // rows

    def spec(height, width):
        return pl.BlockSpec((height, width), lambda i: (i, 0))

    return pl.pallas_call(
        attention_kernel,
        grid=(rows // SPAN,),
        out_shape=(
            jax.ShapeDtypeStruct(queries.shape, jnp.bfloat16),
            jax.ShapeDtypeStruct(kv.shape, jnp.bfloat16),
        ),
        in_specs=[spec(SPAN, d_part), spec(SPAN, d_part), spec(keys_rows, 2 * d_part)],
        out_specs=(spec(SPAN, d_part), spec(keys_rows, 2 * d_part)),
        compiler_params=pltpu.CompilerParams(vmem_limit_bytes=40 * 1024 * 1024),
    )(queries, grads, kv)


def shards(queries, encoded, enc_gain, w_kv, neighbour_block, grad_context):
    n_seq = lax.axis_size("seq")
    device = lax.axis_index("seq")
    per_dev, nlen, ew_part = encoded.shape
    ew_full = ew_part * lax.axis_size("head")
    tok_rows, d_part = queries.shape
    blocks_dev = tok_rows // SPAN
    slot_cap = (per_dev + n_seq - 1) // n_seq
    x_part = encoded.astype(jnp.float32)
    squares = lax.psum(jnp.sum(x_part * x_part, axis=-1), "head")
    inv_rms = lax.rsqrt(squares / ew_full + 1e-05)[..., None]
    normed = (x_part * inv_rms * enc_gain).astype(jnp.bfloat16)
    send_select, recv_select, send_target, back_row = routing(
        neighbour_block, device, n_seq, per_dev, blocks_dev, slot_cap
    )
    width_row = nlen * ew_part
    outgoing = jnp.dot(
        send_select, normed.reshape(per_dev, width_row), preferred_element_type=jnp.float32
    )
    outgoing = outgoing.astype(jnp.bfloat16).reshape(n_seq, slot_cap * width_row)
    incoming = lax.all_to_all(outgoing, "seq", split_axis=0, concat_axis=0, tiled=True)
    gathered = jnp.dot(
        recv_select,
        incoming.reshape(n_seq * slot_cap, width_row),
        preferred_element_type=jnp.float32,
    )
    owned = gathered.astype(jnp.bfloat16).reshape(per_dev, nlen, ew_part)
    full_rows = lax.all_gather(owned, "head", axis=2, tiled=True).reshape(per_dev * nlen, ew_full)
    flat = w_kv.reshape(w_kv.shape[0], 2 * d_part)
    weights = gather_weights(flat).reshape(ew_full, 2 * d_part)
    kv = jnp.dot(full_rows, weights, preferred_element_type=jnp.float32).astype(jnp.bfloat16)
    grad_queries, grad_kv = attention(queries, grad_context, kv)
    partial_rows = lax.dot_general(
        grad_kv, weights, (((1,), (1,)), ((), ())), preferred_element_type=jnp.float32
    )
    grad_encoded = tail(
        back_row,
        send_target,
        partial_rows.reshape(per_dev, nlen, ew_full),
        encoded,
        inv_rms,
        enc_gain[None, :],
    )
    return (grad_queries, grad_encoded)


def solution(mesh):
    return jax.shard_map(
        shards,
        mesh=mesh,
        in_specs=(
            P("seq", "head"),
            P("seq", None, "head"),
            P("head"),
            P("seq", None, "head"),
            P(),
            P("seq", "head"),
        ),
        out_specs=(P("seq", "head"), P("seq", None, "head")),
        check_vma=False,
    )
```

```python
import functools

import jax
import jax.numpy as jnp
from jax import lax
from jax.experimental import pallas as pl
from jax.experimental.pallas import tpu as pltpu
from jax.sharding import PartitionSpec as P

HEAD_DIM = 128
SPAN = 64
NB = 2


def greet(n, heads, me, hd):
    barrier = pltpu.get_barrier_semaphore()
    for d in range(1, n):
        pl.semaphore_signal(
            barrier,
            inc=1,
            device_id={"seq": lax.rem(me + d, n)},
            device_id_type=pl.DeviceIdType.MESH,
        )
    for d in range(1, heads):
        pl.semaphore_signal(
            barrier,
            inc=1,
            device_id={"head": lax.rem(hd + d, heads)},
            device_id_type=pl.DeviceIdType.MESH,
        )
    pl.semaphore_wait(barrier, n + heads - 2)


def remote(src, dst, send, recv, **place):
    return pltpu.make_async_remote_copy(
        src_ref=src,
        dst_ref=dst,
        send_sem=send,
        recv_sem=recv,
        device_id=place,
        device_id_type=pl.DeviceIdType.MESH,
    )


def fold(values):
    total = values[:, :HEAD_DIM]
    for k in range(1, values.shape[1] // HEAD_DIM):
        total = total + values[:, k * HEAD_DIM : (k + 1) * HEAD_DIM]
    return total


def tail_kernel(
    n, heads, back_ref, take_ref, partial_ref, x_ref, rms_ref, gain_ref, out_ref,
    own, land, owned, packed, arrived, mine, others,
    own_sem, rs_send, rs_recv, a_send, a_recv, s_send, s_recv,
):
    me, hd = lax.axis_index("seq"), lax.axis_index("head")
    per_dev, nlen, ew_part = x_ref.shape
    cap = packed.shape[0] // n
    greet(n, heads, me, hd)

    def piece(which):
        return partial_ref.at[:, :, pl.ds(pl.multiple_of(which * ew_part, ew_part), ew_part)]

    sums = []
    for d in range(1, heads):
        to = lax.rem(hd + d, heads)
        sums.append(
            remote(piece(to), land.at[d - 1], rs_send.at[d - 1], rs_recv.at[d - 1], head=to)
        )
        sums[-1].start()
    local = pltpu.make_async_copy(piece(hd), own, own_sem)
    local.start()
    local.wait()
    for item in sums:
        item.wait_recv()

    @pl.loop(0, per_dev)
    def _(r):
        total = own[r]
        for d in range(1, heads):
            total = total + land[d - 1, r]
        owned[r] = total.astype(jnp.bfloat16)

    def parcel(d):
        to = lax.rem(me + d, n)
        return remote(
            packed.at[pl.ds(to * cap, cap)],
            arrived.at[pl.ds(me * cap, cap)],
            a_send.at[d - 1],
            a_recv.at[d - 1],
            seq=to,
        )

    for d in range(1, n):
        to = lax.rem(me + d, n)
        for t in range(cap):
            packed[to * cap + t] = owned[back_ref[to * cap + t]]
        parcel(d).start()
    for t in range(cap):
        arrived[me * cap + t] = owned[back_ref[me * cap + t]]
    for d in range(1, n):
        parcel(d).wait_recv()

    gain = gain_ref[...]

    @pl.loop(0, per_dev)
    def _(i):
        scaled = gain * arrived[take_ref[i]].astype(jnp.float32)
        mine[i] = fold(x_ref[i].astype(jnp.float32) * scaled)

    inners = []
    for d in range(1, heads):
        to = lax.rem(hd + d, heads)
        inners.append(remote(mine, others.at[d - 1], s_send.at[d - 1], s_recv.at[d - 1], head=to))
        inners[-1].start()
    for item in inners:
        item.wait_recv()

    @pl.loop(0, per_dev)
    def _(i):
        total = mine[i]
        for d in range(1, heads):
            total = total + others[d - 1, i]
        inner = jnp.sum(total, axis=-1, keepdims=True) / (ew_part * heads)
        scaled = gain * arrived[take_ref[i]].astype(jnp.float32)
        rms = rms_ref[i]
        x = x_ref[i].astype(jnp.float32)
        out_ref[i] = (rms * scaled - x * (rms * rms * rms * inner)).astype(jnp.bfloat16)

    for item in sums + inners:
        item.wait_send()
    for d in range(1, n):
        parcel(d).wait_send()


def tail(back, take, partial, x, rms, gain):
    n, heads = lax.axis_size("seq"), lax.axis_size("head")
    per_dev, nlen, ew_part = x.shape
    vmem = pl.BlockSpec(memory_space=pltpu.VMEM)
    smem = pl.BlockSpec(memory_space=pltpu.SMEM)
    slots = back.shape[0]
    return pl.pallas_call(
        functools.partial(tail_kernel, n, heads),
        out_shape=jax.ShapeDtypeStruct(x.shape, jnp.bfloat16),
        in_specs=[smem, smem, pl.BlockSpec(memory_space=pl.ANY), vmem, vmem, vmem],
        out_specs=vmem,
        scratch_shapes=[
            pltpu.VMEM(x.shape, jnp.float32),
            pltpu.VMEM((heads - 1,) + x.shape, jnp.float32),
            pltpu.VMEM(x.shape, jnp.bfloat16),
            pltpu.VMEM((slots, nlen, ew_part), jnp.bfloat16),
            pltpu.VMEM((slots, nlen, ew_part), jnp.bfloat16),
            pltpu.VMEM((per_dev, nlen, HEAD_DIM), jnp.float32),
            pltpu.VMEM((heads - 1, per_dev, nlen, HEAD_DIM), jnp.float32),
            pltpu.SemaphoreType.DMA,
            pltpu.SemaphoreType.DMA((heads - 1,)),
            pltpu.SemaphoreType.DMA((heads - 1,)),
            pltpu.SemaphoreType.DMA((n - 1,)),
            pltpu.SemaphoreType.DMA((n - 1,)),
            pltpu.SemaphoreType.DMA((heads - 1,)),
            pltpu.SemaphoreType.DMA((heads - 1,)),
        ],
        compiler_params=pltpu.CompilerParams(
            collective_id=1, has_side_effects=True, vmem_limit_bytes=32 * 1024 * 1024
        ),
    )(back, take, partial, x, rms, gain)


def routing(neighbour_block, device, n_seq, per_dev, blocks_dev, slot_cap):
    count_all = neighbour_block.shape[0]
    index = jnp.arange(count_all, dtype=jnp.int32)
    source = index // per_dev
    holder = neighbour_block // blocks_dev
    earlier = index[None, :] < index[:, None]
    same_pair = jnp.logical_and(
        source[:, None] == source[None, :], holder[:, None] == holder[None, :]
    )
    slot_rank = jnp.sum(jnp.logical_and(same_pair, earlier), axis=1)
    block_rank = jnp.sum(
        jnp.logical_and(neighbour_block[:, None] == neighbour_block[None, :], earlier), axis=1
    )
    row_here = (neighbour_block - device * blocks_dev) * NB + block_rank
    mine_here = holder == device
    rows_local = jnp.arange(per_dev, dtype=jnp.int32)
    slots_all = jnp.arange(n_seq * slot_cap, dtype=jnp.int32)
    select_all = jnp.logical_and(
        rows_local[:, None] == row_here[None, :], mine_here[None, :]
    ).astype(jnp.bfloat16)
    slot_table = ((source * slot_cap + slot_rank)[:, None] == slots_all[None, :]).astype(
        jnp.bfloat16
    )
    recv_select = jnp.dot(select_all, slot_table, preferred_element_type=jnp.float32).astype(
        jnp.bfloat16
    )
    send_target = lax.dynamic_slice_in_dim(holder * slot_cap + slot_rank, device * per_dev, per_dev)
    sent = slots_all[:, None] == send_target[None, :]
    send_row = jnp.sum(jnp.where(sent, rows_local[None, :], 0), axis=1, dtype=jnp.int32)
    take_row = jnp.sum(
        recv_select.astype(jnp.int32) * slots_all[None, :], axis=1, dtype=jnp.int32
    )
    back_row = jnp.sum(
        recv_select.astype(jnp.int32) * rows_local[:, None], axis=0, dtype=jnp.int32
    )
    return (send_row, take_row, send_target.astype(jnp.int32), back_row)


ACROSS = 4
CORES = 2


def gather_kernel(
    n, heads, send_ref, take_ref, w_ref, x_ref, gain_ref, out_ref, full_ref, rms_ref,
    mine, others, normed, packed, incoming, owned,
    own_sem, send_sem, recv_sem, s_send, s_recv, a_send, a_recv, h_own, h_send, h_recv,
):
    me, hd = lax.axis_index("seq"), lax.axis_index("head")
    per_dev, nlen, ew_part = x_ref.shape
    cap = packed.shape[0] // n
    wide = n // (ACROSS * CORES)
    c = lax.rem(me, CORES)
    b = lax.rem(me // CORES, wide)
    a = me // (CORES * wide)

    def at(aa, bb, cc):
        return (aa * wide + bb) * CORES + cc

    greet(n, heads, me, hd)

    def copy(slot, way, target, own):
        return pltpu.make_async_remote_copy(
            src_ref=w_ref if own else out_ref.at[slot],
            dst_ref=out_ref.at[slot],
            send_sem=send_sem.at[way, slot],
            recv_sem=recv_sem.at[slot],
            device_id={"seq": target},
            device_id_type=pl.DeviceIdType.MESH,
        )

    def moves(aa, bb, from_a, from_b, own, act):
        slot = at(aa, bb, c)
        if from_b == 0:
            if from_a >= 0:

                @pl.when(a + 1 < ACROSS)
                def _():
                    act(copy(slot, 0, at(a + 1, b, c), own))

            if from_a <= 0:

                @pl.when(a > 0)
                def _():
                    act(copy(slot, 1, at(a - 1, b, c), own))

        if from_b >= 0:

            @pl.when(b + 1 < wide)
            def _():
                act(copy(slot, 2, at(a, b + 1, c), own))

        if from_b <= 0:

            @pl.when(b > 0)
            def _():
                act(copy(slot, 3, at(a, b - 1, c), own))

        act(copy(slot, 4, at(a, b, 1 - c), own))

    def start(item):
        item.start()

    def wait_recv(slot):
        copy(slot, 4, at(a, b, 1 - c), False).wait_recv()

    def visit(each):
        for t in range(1, ACROSS + wide - 1):
            for j in range(0, min(t, wide - 1) + 1):
                k = t - j
                if k > ACROSS - 1:
                    continue
                for sa in (1, -1) if k else (0,):
                    for sb in (1, -1) if j else (0,):
                        aa, bb = a - sa * k, b - sb * j
                        here = None
                        if sa:
                            here = aa >= 0 if sa > 0 else aa < ACROSS
                        if sb:
                            more = bb >= 0 if sb > 0 else bb < wide
                            here = more if here is None else jnp.logical_and(here, more)

                        @pl.when(here)
                        def _(aa=aa, bb=bb, sa=sa, sb=sb):
                            each(aa, bb, sa, sb)

    own_copy = pltpu.make_async_copy(w_ref, out_ref.at[me], own_sem)
    moves(a, b, 0, 0, True, start)
    own_copy.start()

    @pl.loop(0, per_dev)
    def _(i):
        x = x_ref[i].astype(jnp.float32)
        mine[i] = fold(x * x)

    squares = []
    for d in range(1, heads):
        to = lax.rem(hd + d, heads)
        squares.append(remote(mine, others.at[d - 1], s_send.at[d - 1], s_recv.at[d - 1], head=to))
        squares[-1].start()
    for item in squares:
        item.wait_recv()
    gain = gain_ref[...]

    @pl.loop(0, per_dev)
    def _(i):
        total = mine[i]
        for d in range(1, heads):
            total = total + others[d - 1, i]
        mean = jnp.sum(total, axis=-1, keepdims=True) / (ew_part * heads)
        rms = lax.rsqrt(mean + 1e-05)
        rms_ref[i] = rms
        normed[i] = (x_ref[i].astype(jnp.float32) * rms * gain).astype(jnp.bfloat16)

    def parcel(d):
        to = lax.rem(me + d, n)
        return remote(
            packed.at[pl.ds(to * cap, cap)],
            incoming.at[pl.ds(me * cap, cap)],
            a_send.at[d - 1],
            a_recv.at[d - 1],
            seq=to,
        )

    for d in range(1, n):
        to = lax.rem(me + d, n)
        for t in range(cap):
            packed[to * cap + t] = normed[send_ref[to * cap + t]]
        parcel(d).start()
    for t in range(cap):
        incoming[me * cap + t] = normed[send_ref[me * cap + t]]

    def forward(aa, bb, sa, sb):
        wait_recv(at(aa, bb, c))
        moves(aa, bb, sa, sb, False, start)

    visit(forward)
    for d in range(1, n):
        parcel(d).wait_recv()

    @pl.loop(0, per_dev)
    def _(r):
        owned[r] = incoming[take_ref[r]]

    columns = full_ref.at[:, :, pl.ds(pl.multiple_of(hd * ew_part, ew_part), ew_part)]
    shares = []
    for d in range(1, heads):
        to = lax.rem(hd + d, heads)
        shares.append(remote(owned, columns, h_send.at[d - 1], h_recv.at[d - 1], head=to))
        shares[-1].start()
    own_share = pltpu.make_async_copy(owned, columns, h_own)
    own_share.start()
    for aa in range(ACROSS):
        for bb in range(wide):
            wait_recv(at(aa, bb, 1 - c))
    own_copy.wait()
    own_share.wait()
    for item in shares:
        item.wait_recv()
    for item in squares + shares:
        item.wait_send()
    for d in range(1, n):
        parcel(d).wait_send()
    moves(a, b, 0, 0, True, lambda item: item.wait_send())
    visit(lambda aa, bb, sa, sb: moves(aa, bb, sa, sb, False, lambda item: item.wait_send()))


def gather(send_row, take_row, weights, x, gain):
    n, heads = lax.axis_size("seq"), lax.axis_size("head")
    per_dev, nlen, ew_part = x.shape
    slots = send_row.shape[0]
    vmem = pl.BlockSpec(memory_space=pltpu.VMEM)
    smem = pl.BlockSpec(memory_space=pltpu.SMEM)
    anywhere = pl.BlockSpec(memory_space=pl.ANY)
    return pl.pallas_call(
        functools.partial(gather_kernel, n, heads),
        out_shape=(
            jax.ShapeDtypeStruct((n,) + weights.shape, weights.dtype),
            jax.ShapeDtypeStruct((per_dev, nlen, ew_part * heads), jnp.bfloat16),
            jax.ShapeDtypeStruct((per_dev, nlen, 1), jnp.float32),
        ),
        in_specs=[smem, smem, anywhere, vmem, vmem],
        out_specs=(anywhere, anywhere, vmem),
        scratch_shapes=[
            pltpu.VMEM((per_dev, nlen, HEAD_DIM), jnp.float32),
            pltpu.VMEM((heads - 1, per_dev, nlen, HEAD_DIM), jnp.float32),
            pltpu.VMEM(x.shape, jnp.bfloat16),
            pltpu.VMEM((slots, nlen, ew_part), jnp.bfloat16),
            pltpu.VMEM((slots, nlen, ew_part), jnp.bfloat16),
            pltpu.VMEM(x.shape, jnp.bfloat16),
            pltpu.SemaphoreType.DMA,
            pltpu.SemaphoreType.DMA((5, n)),
            pltpu.SemaphoreType.DMA((n,)),
            pltpu.SemaphoreType.DMA((heads - 1,)),
            pltpu.SemaphoreType.DMA((heads - 1,)),
            pltpu.SemaphoreType.DMA((n - 1,)),
            pltpu.SemaphoreType.DMA((n - 1,)),
            pltpu.SemaphoreType.DMA,
            pltpu.SemaphoreType.DMA((heads - 1,)),
            pltpu.SemaphoreType.DMA((heads - 1,)),
        ],
        compiler_params=pltpu.CompilerParams(
            collective_id=0, has_side_effects=True, vmem_limit_bytes=32 * 1024 * 1024
        ),
    )(send_row, take_row, weights, x, gain)


GROUP = 4


def attention_kernel(q_ref, g_ref, kv_ref, gq_ref, gkv_ref):
    d_part = q_ref.shape[1]
    pair = 2 * HEAD_DIM
    scale = 1.0 / HEAD_DIM**0.5
    nt = (((1,), (1,)), ((), ()))
    tn = (((0,), (0,)), ((), ()))
    dot = functools.partial(lax.dot_general, preferred_element_type=jnp.float32)

    def diagonal(x):
        blank = jnp.zeros((x.shape[0], HEAD_DIM), x.dtype)
        upper = jnp.concatenate([x[:, :HEAD_DIM], blank], axis=1)
        lower = jnp.concatenate([blank, x[:, HEAD_DIM:]], axis=1)
        return jnp.concatenate([upper, lower], axis=0)

    @pl.loop(0, d_part // (GROUP * pair))
    def _(step):
        cols, cols_v = [], []
        for h in range(GROUP):
            start = pl.multiple_of((step * GROUP + h) * pair, pair)
            cols.append(pl.ds(start, pair))
            cols_v.append(pl.ds(pl.multiple_of(start + d_part, pair), pair))
        queries = [diagonal(q_ref[:, c]) for c in cols]
        grads = [diagonal(g_ref[:, c]) for c in cols]
        keys = [kv_ref[:, c] for c in cols]
        values = [kv_ref[:, c] for c in cols_v]
        scores = [dot(k, q, nt) * scale for k, q in zip(keys, queries)]
        dprobs = [dot(v, g, nt) for v, g in zip(values, grads)]
        low, dscores = [], []
        for s, dp in zip(scores, dprobs):
            weight = jnp.exp(s - jnp.max(s, axis=0, keepdims=True))
            probs = weight / jnp.sum(weight, axis=0, keepdims=True)
            delta = jnp.sum(probs * dp, axis=0, keepdims=True)
            low.append(probs.astype(jnp.bfloat16))
            dscores.append((probs * (dp - delta)).astype(jnp.bfloat16))
        grad_k = [dot(d, q, (((1,), (0,)), ((), ()))) * scale for d, q in zip(dscores, queries)]
        grad_v = [dot(p, g, (((1,), (0,)), ((), ()))) for p, g in zip(low, grads)]
        grad_q = [dot(d, k, tn) * scale for d, k in zip(dscores, keys)]
        for h in range(GROUP):
            gkv_ref[:, cols[h]] = grad_k[h].astype(jnp.bfloat16)
            gkv_ref[:, cols_v[h]] = grad_v[h].astype(jnp.bfloat16)
            both = jnp.concatenate(
                [grad_q[h][:SPAN, :HEAD_DIM], grad_q[h][SPAN:, HEAD_DIM:]], axis=1
            )
            gq_ref[:, cols[h]] = both.astype(jnp.bfloat16)


def attention(queries, grads, kv):
    rows, d_part = queries.shape
    keys_rows = kv.shape[0] * SPAN // rows

    def spec(height, width):
        return pl.BlockSpec((height, width), lambda i: (i, 0))

    return pl.pallas_call(
        attention_kernel,
        grid=(rows // SPAN,),
        out_shape=(
            jax.ShapeDtypeStruct(queries.shape, jnp.bfloat16),
            jax.ShapeDtypeStruct(kv.shape, jnp.bfloat16),
        ),
        in_specs=[spec(SPAN, d_part), spec(SPAN, d_part), spec(keys_rows, 2 * d_part)],
        out_specs=(spec(SPAN, d_part), spec(keys_rows, 2 * d_part)),
        compiler_params=pltpu.CompilerParams(vmem_limit_bytes=40 * 1024 * 1024),
    )(queries, grads, kv)


def shards(queries, encoded, enc_gain, w_kv, neighbour_block, grad_context):
    n_seq = lax.axis_size("seq")
    device = lax.axis_index("seq")
    per_dev, nlen, ew_part = encoded.shape
    ew_full = ew_part * lax.axis_size("head")
    tok_rows, d_part = queries.shape
    blocks_dev = tok_rows // SPAN
    slot_cap = (per_dev + n_seq - 1) // n_seq
    send_row, take_row, send_target, back_row = routing(
        neighbour_block, device, n_seq, per_dev, blocks_dev, slot_cap
    )
    flat = w_kv.reshape(w_kv.shape[0], 2 * d_part)
    weights, owned, inv_rms = gather(send_row, take_row, flat, encoded, enc_gain[None, :])
    weights = weights.reshape(ew_full, 2 * d_part)
    full_rows = owned.reshape(per_dev * nlen, ew_full)
    kv = jnp.dot(full_rows, weights, preferred_element_type=jnp.float32).astype(jnp.bfloat16)
    grad_queries, grad_kv = attention(queries, grad_context, kv)
    partial_rows = lax.dot_general(
        grad_kv, weights, (((1,), (1,)), ((), ())), preferred_element_type=jnp.float32
    )
    grad_encoded = tail(
        back_row,
        send_target,
        partial_rows.reshape(per_dev, nlen, ew_full),
        encoded,
        inv_rms,
        enc_gain[None, :],
    )
    return (grad_queries, grad_encoded)


def solution(mesh):
    return jax.shard_map(
        shards,
        mesh=mesh,
        in_specs=(
            P("seq", "head"),
            P("seq", None, "head"),
            P("head"),
            P("seq", None, "head"),
            P(),
            P("seq", "head"),
        ),
        out_specs=(P("seq", "head"), P("seq", None, "head")),
        check_vma=False,
    )
```

```python
import functools

import jax
import jax.numpy as jnp
from jax import lax
from jax.experimental import pallas as pl
from jax.experimental.pallas import tpu as pltpu
from jax.sharding import PartitionSpec as P

HEAD_DIM = 128
SPAN = 64
NB = 2


def greet(n, heads, me, hd):
    barrier = pltpu.get_barrier_semaphore()
    for d in range(1, n):
        pl.semaphore_signal(
            barrier,
            inc=1,
            device_id={"seq": lax.rem(me + d, n)},
            device_id_type=pl.DeviceIdType.MESH,
        )
    for d in range(1, heads):
        pl.semaphore_signal(
            barrier,
            inc=1,
            device_id={"head": lax.rem(hd + d, heads)},
            device_id_type=pl.DeviceIdType.MESH,
        )
    pl.semaphore_wait(barrier, n + heads - 2)


def remote(src, dst, send, recv, **place):
    return pltpu.make_async_remote_copy(
        src_ref=src,
        dst_ref=dst,
        send_sem=send,
        recv_sem=recv,
        device_id=place,
        device_id_type=pl.DeviceIdType.MESH,
    )


def fold(values):
    total = values[:, :HEAD_DIM]
    for k in range(1, values.shape[1] // HEAD_DIM):
        total = total + values[:, k * HEAD_DIM : (k + 1) * HEAD_DIM]
    return total


def tail_kernel(
    n, heads, back_ref, take_ref, partial_ref, x_ref, rms_ref, gain_ref, out_ref,
    own, land, owned, packed, arrived, mine, others,
    own_sem, rs_send, rs_recv, a_send, a_recv, s_send, s_recv,
):
    me, hd = lax.axis_index("seq"), lax.axis_index("head")
    per_dev, nlen, ew_part = x_ref.shape
    cap = packed.shape[0] // n
    greet(n, heads, me, hd)

    def piece(which):
        return partial_ref.at[:, :, pl.ds(pl.multiple_of(which * ew_part, ew_part), ew_part)]

    sums = []
    for d in range(1, heads):
        to = lax.rem(hd + d, heads)
        sums.append(
            remote(piece(to), land.at[d - 1], rs_send.at[d - 1], rs_recv.at[d - 1], head=to)
        )
        sums[-1].start()
    local = pltpu.make_async_copy(piece(hd), own, own_sem)
    local.start()
    local.wait()
    for item in sums:
        item.wait_recv()

    @pl.loop(0, per_dev)
    def _(r):
        total = own[r]
        for d in range(1, heads):
            total = total + land[d - 1, r]
        owned[r] = total.astype(jnp.bfloat16)

    def parcel(d):
        to = lax.rem(me + d, n)
        return remote(
            packed.at[pl.ds(to * cap, cap)],
            arrived.at[pl.ds(me * cap, cap)],
            a_send.at[d - 1],
            a_recv.at[d - 1],
            seq=to,
        )

    for d in range(1, n):
        to = lax.rem(me + d, n)
        for t in range(cap):
            packed[to * cap + t] = owned[back_ref[to * cap + t]]
        parcel(d).start()
    for t in range(cap):
        arrived[me * cap + t] = owned[back_ref[me * cap + t]]
    for d in range(1, n):
        parcel(d).wait_recv()

    gain = gain_ref[...]
    mine[...] = jnp.zeros_like(mine)

    @pl.loop(0, per_dev)
    def _(i):
        scaled = gain * arrived[take_ref[i]].astype(jnp.float32)
        put_column(mine, i, fold(x_ref[i].astype(jnp.float32) * scaled))

    inners = []
    for d in range(1, heads):
        to = lax.rem(hd + d, heads)
        inners.append(remote(mine, others.at[d - 1], s_send.at[d - 1], s_recv.at[d - 1], head=to))
        inners[-1].start()
    for item in inners:
        item.wait_recv()

    @pl.loop(0, per_dev)
    def _(i):
        total = mine[...]
        for d in range(1, heads):
            total = total + others[d - 1]
        inner = column(total, i) / (ew_part * heads)
        scaled = gain * arrived[take_ref[i]].astype(jnp.float32)
        rms = rms_ref[i]
        x = x_ref[i].astype(jnp.float32)
        out_ref[i] = (rms * scaled - x * (rms * rms * rms * inner)).astype(jnp.bfloat16)

    for item in sums + inners:
        item.wait_send()
    for d in range(1, n):
        parcel(d).wait_send()


def tail(back, take, partial, x, rms, gain):
    n, heads = lax.axis_size("seq"), lax.axis_size("head")
    per_dev, nlen, ew_part = x.shape
    vmem = pl.BlockSpec(memory_space=pltpu.VMEM)
    smem = pl.BlockSpec(memory_space=pltpu.SMEM)
    slots = back.shape[0]
    return pl.pallas_call(
        functools.partial(tail_kernel, n, heads),
        out_shape=jax.ShapeDtypeStruct(x.shape, jnp.bfloat16),
        in_specs=[smem, smem, pl.BlockSpec(memory_space=pl.ANY), vmem, vmem, vmem],
        out_specs=vmem,
        scratch_shapes=[
            pltpu.VMEM(x.shape, jnp.float32),
            pltpu.VMEM((heads - 1,) + x.shape, jnp.float32),
            pltpu.VMEM(x.shape, jnp.bfloat16),
            pltpu.VMEM((slots, nlen, ew_part), jnp.bfloat16),
            pltpu.VMEM((slots, nlen, ew_part), jnp.bfloat16),
            pltpu.VMEM((nlen, HEAD_DIM), jnp.float32),
            pltpu.VMEM((heads - 1, nlen, HEAD_DIM), jnp.float32),
            pltpu.SemaphoreType.DMA,
            pltpu.SemaphoreType.DMA((heads - 1,)),
            pltpu.SemaphoreType.DMA((heads - 1,)),
            pltpu.SemaphoreType.DMA((n - 1,)),
            pltpu.SemaphoreType.DMA((n - 1,)),
            pltpu.SemaphoreType.DMA((heads - 1,)),
            pltpu.SemaphoreType.DMA((heads - 1,)),
        ],
        compiler_params=pltpu.CompilerParams(
            collective_id=1, has_side_effects=True, vmem_limit_bytes=32 * 1024 * 1024
        ),
    )(back, take, partial, x, rms, gain)


def routing(neighbour_block, device, n_seq, per_dev, blocks_dev, slot_cap):
    count_all = neighbour_block.shape[0]
    index = jnp.arange(count_all, dtype=jnp.int32)
    source = index // per_dev
    holder = neighbour_block // blocks_dev
    earlier = index[None, :] < index[:, None]
    same_pair = jnp.logical_and(
        source[:, None] == source[None, :], holder[:, None] == holder[None, :]
    )
    slot_rank = jnp.sum(jnp.logical_and(same_pair, earlier), axis=1)
    block_rank = jnp.sum(
        jnp.logical_and(neighbour_block[:, None] == neighbour_block[None, :], earlier), axis=1
    )
    row_here = (neighbour_block - device * blocks_dev) * NB + block_rank
    mine_here = holder == device
    rows_local = jnp.arange(per_dev, dtype=jnp.int32)
    slots_all = jnp.arange(n_seq * slot_cap, dtype=jnp.int32)
    select_all = jnp.logical_and(
        rows_local[:, None] == row_here[None, :], mine_here[None, :]
    ).astype(jnp.bfloat16)
    slot_table = ((source * slot_cap + slot_rank)[:, None] == slots_all[None, :]).astype(
        jnp.bfloat16
    )
    recv_select = jnp.dot(select_all, slot_table, preferred_element_type=jnp.float32).astype(
        jnp.bfloat16
    )
    send_target = lax.dynamic_slice_in_dim(holder * slot_cap + slot_rank, device * per_dev, per_dev)
    sent = slots_all[:, None] == send_target[None, :]
    send_row = jnp.sum(jnp.where(sent, rows_local[None, :], 0), axis=1, dtype=jnp.int32)
    take_row = jnp.sum(
        recv_select.astype(jnp.int32) * slots_all[None, :], axis=1, dtype=jnp.int32
    )
    back_row = jnp.sum(
        recv_select.astype(jnp.int32) * rows_local[:, None], axis=0, dtype=jnp.int32
    )
    return (send_row, take_row, send_target.astype(jnp.int32), back_row)


ACROSS = 4
CORES = 2


def put_column(ref, i, values):
    lane = lax.broadcasted_iota(jnp.int32, ref.shape, 1)
    ref[...] = jnp.where(lane == i, jnp.sum(values, axis=-1, keepdims=True), ref[...])


def column(total, i):
    lane = lax.broadcasted_iota(jnp.int32, total.shape, 1)
    return jnp.sum(jnp.where(lane == i, total, 0.0), axis=-1, keepdims=True)


def gather_kernel(
    n, heads, send_ref, take_ref, w_ref, x_ref, gain_ref, out_ref, full_ref, rms_ref,
    mine, others, normed, packed, incoming, owned,
    own_sem, send_sem, recv_sem, s_send, s_recv, a_send, a_recv, h_own, h_send, h_recv,
):
    me, hd = lax.axis_index("seq"), lax.axis_index("head")
    per_dev, nlen, ew_part = x_ref.shape
    cap = packed.shape[0] // n
    wide = n // (ACROSS * CORES)
    c = lax.rem(me, CORES)
    b = lax.rem(me // CORES, wide)
    a = me // (CORES * wide)

    def at(aa, bb, cc):
        return (aa * wide + bb) * CORES + cc

    greet(n, heads, me, hd)

    def copy(slot, way, target, own):
        return pltpu.make_async_remote_copy(
            src_ref=w_ref if own else out_ref.at[slot],
            dst_ref=out_ref.at[slot],
            send_sem=send_sem.at[way, slot],
            recv_sem=recv_sem.at[slot],
            device_id={"seq": target},
            device_id_type=pl.DeviceIdType.MESH,
        )

    def moves(aa, bb, from_a, from_b, own, act):
        slot = at(aa, bb, c)
        if from_b == 0:
            if from_a >= 0:

                @pl.when(a + 1 < ACROSS)
                def _():
                    act(copy(slot, 0, at(a + 1, b, c), own))

            if from_a <= 0:

                @pl.when(a > 0)
                def _():
                    act(copy(slot, 1, at(a - 1, b, c), own))

        if from_b >= 0:

            @pl.when(b + 1 < wide)
            def _():
                act(copy(slot, 2, at(a, b + 1, c), own))

        if from_b <= 0:

            @pl.when(b > 0)
            def _():
                act(copy(slot, 3, at(a, b - 1, c), own))

        act(copy(slot, 4, at(a, b, 1 - c), own))

    def start(item):
        item.start()

    def wait_recv(slot):
        copy(slot, 4, at(a, b, 1 - c), False).wait_recv()

    def visit(each):
        for t in range(1, ACROSS + wide - 1):
            for j in range(0, min(t, wide - 1) + 1):
                k = t - j
                if k > ACROSS - 1:
                    continue
                for sa in (1, -1) if k else (0,):
                    for sb in (1, -1) if j else (0,):
                        aa, bb = a - sa * k, b - sb * j
                        here = None
                        if sa:
                            here = aa >= 0 if sa > 0 else aa < ACROSS
                        if sb:
                            more = bb >= 0 if sb > 0 else bb < wide
                            here = more if here is None else jnp.logical_and(here, more)

                        @pl.when(here)
                        def _(aa=aa, bb=bb, sa=sa, sb=sb):
                            each(aa, bb, sa, sb)

    own_copy = pltpu.make_async_copy(w_ref, out_ref.at[me], own_sem)
    moves(a, b, 0, 0, True, start)
    own_copy.start()

    mine[...] = jnp.zeros_like(mine)

    @pl.loop(0, per_dev)
    def _(i):
        x = x_ref[i].astype(jnp.float32)
        put_column(mine, i, fold(x * x))

    squares = []
    for d in range(1, heads):
        to = lax.rem(hd + d, heads)
        squares.append(remote(mine, others.at[d - 1], s_send.at[d - 1], s_recv.at[d - 1], head=to))
        squares[-1].start()
    for item in squares:
        item.wait_recv()
    gain = gain_ref[...]

    @pl.loop(0, per_dev)
    def _(i):
        total = mine[...]
        for d in range(1, heads):
            total = total + others[d - 1]
        mean = column(total, i) / (ew_part * heads)
        rms = lax.rsqrt(mean + 1e-05)
        rms_ref[i] = rms
        normed[i] = (x_ref[i].astype(jnp.float32) * rms * gain).astype(jnp.bfloat16)

    def parcel(d):
        to = lax.rem(me + d, n)
        return remote(
            packed.at[pl.ds(to * cap, cap)],
            incoming.at[pl.ds(me * cap, cap)],
            a_send.at[d - 1],
            a_recv.at[d - 1],
            seq=to,
        )

    for d in range(1, n):
        to = lax.rem(me + d, n)
        for t in range(cap):
            packed[to * cap + t] = normed[send_ref[to * cap + t]]
        parcel(d).start()
    for t in range(cap):
        incoming[me * cap + t] = normed[send_ref[me * cap + t]]

    def forward(aa, bb, sa, sb):
        wait_recv(at(aa, bb, c))
        moves(aa, bb, sa, sb, False, start)

    visit(forward)
    for d in range(1, n):
        parcel(d).wait_recv()

    @pl.loop(0, per_dev)
    def _(r):
        owned[r] = incoming[take_ref[r]]

    columns = full_ref.at[:, :, pl.ds(pl.multiple_of(hd * ew_part, ew_part), ew_part)]
    shares = []
    for d in range(1, heads):
        to = lax.rem(hd + d, heads)
        shares.append(remote(owned, columns, h_send.at[d - 1], h_recv.at[d - 1], head=to))
        shares[-1].start()
    own_share = pltpu.make_async_copy(owned, columns, h_own)
    own_share.start()
    for aa in range(ACROSS):
        for bb in range(wide):
            wait_recv(at(aa, bb, 1 - c))
    own_copy.wait()
    own_share.wait()
    for item in shares:
        item.wait_recv()
    for item in squares + shares:
        item.wait_send()
    for d in range(1, n):
        parcel(d).wait_send()
    moves(a, b, 0, 0, True, lambda item: item.wait_send())
    visit(lambda aa, bb, sa, sb: moves(aa, bb, sa, sb, False, lambda item: item.wait_send()))


def gather(send_row, take_row, weights, x, gain):
    n, heads = lax.axis_size("seq"), lax.axis_size("head")
    per_dev, nlen, ew_part = x.shape
    slots = send_row.shape[0]
    vmem = pl.BlockSpec(memory_space=pltpu.VMEM)
    smem = pl.BlockSpec(memory_space=pltpu.SMEM)
    anywhere = pl.BlockSpec(memory_space=pl.ANY)
    return pl.pallas_call(
        functools.partial(gather_kernel, n, heads),
        out_shape=(
            jax.ShapeDtypeStruct((n,) + weights.shape, weights.dtype),
            jax.ShapeDtypeStruct((per_dev, nlen, ew_part * heads), jnp.bfloat16),
            jax.ShapeDtypeStruct((per_dev, nlen, 1), jnp.float32),
        ),
        in_specs=[smem, smem, anywhere, vmem, vmem],
        out_specs=(anywhere, anywhere, vmem),
        scratch_shapes=[
            pltpu.VMEM((nlen, HEAD_DIM), jnp.float32),
            pltpu.VMEM((heads - 1, nlen, HEAD_DIM), jnp.float32),
            pltpu.VMEM(x.shape, jnp.bfloat16),
            pltpu.VMEM((slots, nlen, ew_part), jnp.bfloat16),
            pltpu.VMEM((slots, nlen, ew_part), jnp.bfloat16),
            pltpu.VMEM(x.shape, jnp.bfloat16),
            pltpu.SemaphoreType.DMA,
            pltpu.SemaphoreType.DMA((5, n)),
            pltpu.SemaphoreType.DMA((n,)),
            pltpu.SemaphoreType.DMA((heads - 1,)),
            pltpu.SemaphoreType.DMA((heads - 1,)),
            pltpu.SemaphoreType.DMA((n - 1,)),
            pltpu.SemaphoreType.DMA((n - 1,)),
            pltpu.SemaphoreType.DMA,
            pltpu.SemaphoreType.DMA((heads - 1,)),
            pltpu.SemaphoreType.DMA((heads - 1,)),
        ],
        compiler_params=pltpu.CompilerParams(
            collective_id=0, has_side_effects=True, vmem_limit_bytes=32 * 1024 * 1024
        ),
    )(send_row, take_row, weights, x, gain)


GROUP = 4


def attention_kernel(q_ref, g_ref, kv_ref, gq_ref, gkv_ref):
    d_part = q_ref.shape[1]
    pair = 2 * HEAD_DIM
    scale = 1.0 / HEAD_DIM**0.5
    nt = (((1,), (1,)), ((), ()))
    tn = (((0,), (0,)), ((), ()))
    dot = functools.partial(lax.dot_general, preferred_element_type=jnp.float32)

    def diagonal(x):
        blank = jnp.zeros((x.shape[0], HEAD_DIM), x.dtype)
        upper = jnp.concatenate([x[:, :HEAD_DIM], blank], axis=1)
        lower = jnp.concatenate([blank, x[:, HEAD_DIM:]], axis=1)
        return jnp.concatenate([upper, lower], axis=0)

    @pl.loop(0, d_part // (GROUP * pair))
    def _(step):
        cols, cols_v = [], []
        for h in range(GROUP):
            start = pl.multiple_of((step * GROUP + h) * pair, pair)
            cols.append(pl.ds(start, pair))
            cols_v.append(pl.ds(pl.multiple_of(start + d_part, pair), pair))
        queries = [diagonal(q_ref[:, c]) for c in cols]
        grads = [diagonal(g_ref[:, c]) for c in cols]
        keys = [kv_ref[:, c] for c in cols]
        values = [kv_ref[:, c] for c in cols_v]
        scores = [dot(k, q, nt) * scale for k, q in zip(keys, queries)]
        dprobs = [dot(v, g, nt) for v, g in zip(values, grads)]
        low, dscores = [], []
        for s, dp in zip(scores, dprobs):
            weight = jnp.exp(s - jnp.max(s, axis=0, keepdims=True))
            probs = weight / jnp.sum(weight, axis=0, keepdims=True)
            delta = jnp.sum(probs * dp, axis=0, keepdims=True)
            low.append(probs.astype(jnp.bfloat16))
            dscores.append((probs * (dp - delta)).astype(jnp.bfloat16))
        grad_k = [dot(d, q, (((1,), (0,)), ((), ()))) * scale for d, q in zip(dscores, queries)]
        grad_v = [dot(p, g, (((1,), (0,)), ((), ()))) for p, g in zip(low, grads)]
        grad_q = [dot(d, k, tn) * scale for d, k in zip(dscores, keys)]
        for h in range(GROUP):
            gkv_ref[:, cols[h]] = grad_k[h].astype(jnp.bfloat16)
            gkv_ref[:, cols_v[h]] = grad_v[h].astype(jnp.bfloat16)
            both = jnp.concatenate(
                [grad_q[h][:SPAN, :HEAD_DIM], grad_q[h][SPAN:, HEAD_DIM:]], axis=1
            )
            gq_ref[:, cols[h]] = both.astype(jnp.bfloat16)


def attention(queries, grads, kv):
    rows, d_part = queries.shape
    keys_rows = kv.shape[0] * SPAN // rows

    def spec(height, width):
        return pl.BlockSpec((height, width), lambda i: (i, 0))

    return pl.pallas_call(
        attention_kernel,
        grid=(rows // SPAN,),
        out_shape=(
            jax.ShapeDtypeStruct(queries.shape, jnp.bfloat16),
            jax.ShapeDtypeStruct(kv.shape, jnp.bfloat16),
        ),
        in_specs=[spec(SPAN, d_part), spec(SPAN, d_part), spec(keys_rows, 2 * d_part)],
        out_specs=(spec(SPAN, d_part), spec(keys_rows, 2 * d_part)),
        compiler_params=pltpu.CompilerParams(vmem_limit_bytes=40 * 1024 * 1024),
    )(queries, grads, kv)


def shards(queries, encoded, enc_gain, w_kv, neighbour_block, grad_context):
    n_seq = lax.axis_size("seq")
    device = lax.axis_index("seq")
    per_dev, nlen, ew_part = encoded.shape
    ew_full = ew_part * lax.axis_size("head")
    tok_rows, d_part = queries.shape
    blocks_dev = tok_rows // SPAN
    slot_cap = (per_dev + n_seq - 1) // n_seq
    send_row, take_row, send_target, back_row = routing(
        neighbour_block, device, n_seq, per_dev, blocks_dev, slot_cap
    )
    flat = w_kv.reshape(w_kv.shape[0], 2 * d_part)
    weights, owned, inv_rms = gather(send_row, take_row, flat, encoded, enc_gain[None, :])
    weights = weights.reshape(ew_full, 2 * d_part)
    full_rows = owned.reshape(per_dev * nlen, ew_full)
    kv = jnp.dot(full_rows, weights, preferred_element_type=jnp.float32).astype(jnp.bfloat16)
    grad_queries, grad_kv = attention(queries, grad_context, kv)
    partial_rows = lax.dot_general(
        grad_kv, weights, (((1,), (1,)), ((), ())), preferred_element_type=jnp.float32
    )
    grad_encoded = tail(
        back_row,
        send_target,
        partial_rows.reshape(per_dev, nlen, ew_full),
        encoded,
        inv_rms,
        enc_gain[None, :],
    )
    return (grad_queries, grad_encoded)


def solution(mesh):
    return jax.shard_map(
        shards,
        mesh=mesh,
        in_specs=(
            P("seq", "head"),
            P("seq", None, "head"),
            P("head"),
            P("seq", None, "head"),
            P(),
            P("seq", "head"),
        ),
        out_specs=(P("seq", "head"), P("seq", None, "head")),
        check_vma=False,
    )
```
